512 devices in a mesh: context: 64 (over x, z), tensor: 8 (over y, core).
Axes of the slice: x: 4, y: 4, z: 16, core: 2. Of those that a mesh axis runs over, the one named last changes fastest.
Arguments:
- query: bfloat16 [8192, 2048], P('context', 'tensor'), may hold values from -5 to 5
- key_proj: bfloat16 [8192, 1024], P('context', 'tensor'), may hold values from -5 to 5
- value: bfloat16 [8192, 1024], P('context', 'tensor'), may hold values from -6 to 6
- out_weight: bfloat16 [2048, 4096], P('tensor'), may hold values from -0.125 to 0.125
- grad_out: bfloat16 [8192, 4096], P('context', 'tensor'), may hold values from -6 to 6
- order: int32 [8192], replicated, may hold values from 0 to 8191, each once
- segment: int32 [8192], replicated, may hold values from 0 to 7, never falling along the last dimension, each value on 1 to 2048 neighbouring positions
Outputs:
- output: bfloat16 [8192, 4096], P('context', 'tensor')
- grad_query: bfloat16 [8192, 2048], P('context', 'tensor')
- grad_key: bfloat16 [8192, 1024], P('context', 'tensor')
- grad_value: bfloat16 [8192, 1024], P('context', 'tensor')
The draws below stay inside these ranges and needn't reach their ends.
Inputs may be any that keep to these rules, and one draw needn't show every extreme that they name: `order`: each position once. `segment`: never falls along positions; every document 1 to 2048 positions long.
All inputs are finite; a program needn't handle non-finite values.
Results may differ from the reference program's by a relative error of at most 0.03.
Values may be sent and summed in bfloat16 or wider, within the bound.
A program may use at most 64 MiB of HBM per device.

```python
import math
import jax
import jax.numpy as jnp
import numpy as np
from jax import lax

D = 4096
QH = 16
KVH = 8
HD = 128
DOCS = 8
TOKENS = 8192
DOC_MOST = 2048


def draw_query(key, part):
    key = jax.random.fold_in(key, 1)
    return jnp.clip(jax.random.normal(key, (TOKENS, QH * HD)), -5.0, 5.0).astype(jnp.bfloat16)


def draw_key_proj(key, part):
    key = jax.random.fold_in(key, 2)
    return jnp.clip(jax.random.normal(key, (TOKENS, KVH * HD)), -5.0, 5.0).astype(jnp.bfloat16)


def block_scale(key, shape, shards, least, high):
    level = 1.0
    for dim, parts in shards:
        heights = jax.random.uniform(jax.random.fold_in(jax.random.fold_in(key, 6), dim), (parts,), jnp.float32, least / len(shards), high / len(shards))
        level = level * jnp.repeat(jnp.exp(heights), shape[dim] // parts).reshape((-1,) + (1,) * (len(shape) - 1 - dim))
    return level


def profile(amount, total, bound, skew):
    loads = [(1 << 20) // math.isqrt(grade ** skew) + 1 for grade in range(2, amount + 1)]
    surplus, holding = total - bound - (amount - 1), [1] * (amount - 1)
    while surplus > 0:
        free = [i for i in range(amount - 1) if holding[i] < bound]
        whole, remaining = sum([loads[i] for i in free]), surplus
        for i in free:
            addition = min(bound - holding[i], max(1, remaining * loads[i] // whole), surplus)
            holding[i] = holding[i] + addition
            surplus = surplus - addition
    return np.array([bound] + holding)


def uneven_parts(rng, amount, total, reach, skew):
    if amount == 2:
        one = jax.random.randint(rng, (), max(1, total - reach), min(reach, total - 1) + 1)
        return jnp.stack([one, total - one])
    lengths = jnp.asarray(profile(amount, total, reach, skew), jnp.int32)
    couples = (amount - 1) // 2
    donor, sink = lengths[1:1 + 2 * couples:2], lengths[2:2 + 2 * couples:2]
    margin = jnp.minimum(donor - 1, reach - sink)
    passed = jax.random.randint(jax.random.fold_in(rng, 1), (couples,), 0, 1 << 20) % (margin + 1)
    lengths = lengths.at[1:1 + 2 * couples:2].set(donor - passed).at[2:2 + 2 * couples:2].set(sink + passed)
    return lengths[jax.random.permutation(jax.random.fold_in(rng, 2), amount)]


def scatter_about(rng, extent, spread, limit, shards=(), held_as=jnp.bfloat16):
    values = jax.random.normal(rng, extent, jnp.float32) * spread
    if len(shards) > 0:
        values = block_scale(rng, extent, shards, -0.22, 0.18) * values
    return jnp.clip(values, min=-limit, max=limit).astype(held_as)


def setup_inputs(seed: int = 0) -> dict:
    arg_keys = jax.random.split(jax.random.key(seed), 8)
    query = draw_query(jax.random.fold_in(arg_keys[7], 71), 0)
    key_proj = draw_key_proj(jax.random.fold_in(arg_keys[7], 71), 0)
    value = scatter_about(arg_keys[2], (TOKENS, KVH * HD), 1.0, 6.0, ((0, 64), (1, 8)))
    out_weight = scatter_about(arg_keys[3], (QH * HD, D), (QH * HD) ** -0.5, 0.125, ((0, 8),))
    grad_out = scatter_about(arg_keys[4], (TOKENS, D), 1.0, 6.0, ((0, 64), (1, 8)))
    order = jax.random.permutation(arg_keys[5], TOKENS).astype(jnp.int32)
    segment = jnp.searchsorted(jnp.cumsum(uneven_parts(arg_keys[6], DOCS, TOKENS, DOC_MOST, 0)), jnp.arange(TOKENS), side="right").astype(jnp.int32)
    return {"query": query, "key_proj": key_proj, "value": value, "out_weight": out_weight, "grad_out": grad_out, "order": order, "segment": segment}


NEG = -1e+30

def reference(query, key_proj, value, out_weight, grad_out, order, segment):
    tokens = query.shape[0]
    groups = KVH
    ratio = QH // KVH
    scale = 1.0 / math.sqrt(HD)
    block = math.gcd(tokens, 256)
    blocks = tokens // block
    row_segment = jnp.take(segment, order)
    keys_f = key_proj.reshape(tokens, groups, HD).astype(jnp.float32)
    values_f = value.reshape(tokens, groups, HD).astype(jnp.float32)
    query_blocks = query.reshape(blocks, block, groups, ratio, HD)
    order_blocks = order.reshape(blocks, block)
    segment_blocks = row_segment.reshape(blocks, block)

    def scores_of(query_block, order_block, segment_block):
        mask = (segment_block[:, None] == row_segment[None, :]) & (order[None, :] <= order_block[:, None])
        scores = jnp.einsum('qgrd,kgd->qgrk', query_block.astype(jnp.float32), keys_f) * scale
        return (mask[:, None, None, :], jnp.where(mask[:, None, None, :], scores, NEG))

    def forward_block(inputs):
        query_block, order_block, segment_block = inputs
        mask, scores = scores_of(query_block, order_block, segment_block)
        top = lax.optimization_barrier(jnp.max(scores, axis=-1))
        log_total = top + jnp.log(lax.optimization_barrier(jnp.sum(jnp.exp(scores - top[..., None]), axis=-1)))
        probs = jnp.where(mask, jnp.exp(scores - log_total[..., None]), 0.0).astype(jnp.bfloat16)
        attended = jnp.einsum('qgrk,kgd->qgrd', probs.astype(jnp.float32), values_f).astype(jnp.bfloat16)
        return (attended, log_total)
    attended, log_total = lax.map(forward_block, (query_blocks, order_blocks, segment_blocks))
    attended = attended.reshape(tokens, QH * HD)
    output = jnp.dot(attended, out_weight, preferred_element_type=jnp.float32).astype(jnp.bfloat16)
    grad_attended = jnp.dot(grad_out, out_weight.T, preferred_element_type=jnp.float32).astype(jnp.bfloat16)
    grad_four = grad_attended.reshape(tokens, groups, ratio, HD)
    delta = lax.optimization_barrier(jnp.sum(grad_four.astype(jnp.float32) * attended.reshape(tokens, groups, ratio, HD).astype(jnp.float32), axis=-1))
    grad_blocks = grad_four.reshape(blocks, block, groups, ratio, HD)
    log_blocks = log_total.reshape(blocks, block, groups, ratio)
    delta_blocks = delta.reshape(blocks, block, groups, ratio)

    def backward_block(carry, inputs):
        key_sum, value_sum = carry
        query_block, order_block, segment_block, grad_block, log_block, delta_block = inputs
        mask, scores = scores_of(query_block, order_block, segment_block)
        probs = jnp.where(mask, jnp.exp(scores - log_block[..., None]), 0.0)
        probs_low = probs.astype(jnp.bfloat16)
        grad_probs = jnp.einsum('qgrd,kgd->qgrk', grad_block.astype(jnp.float32), values_f)
        grad_scores = (probs * (grad_probs - delta_block[..., None]) * scale).astype(jnp.bfloat16)
        grad_scores_f = grad_scores.astype(jnp.float32)
        grad_query_block = jnp.einsum('qgrk,kgd->qgrd', grad_scores_f, keys_f).astype(jnp.bfloat16)
        key_sum = key_sum + jnp.einsum('qgrk,qgrd->kgd', grad_scores_f, query_block.astype(jnp.float32))
        value_sum = value_sum + jnp.einsum('qgrk,qgrd->kgd', probs_low.astype(jnp.float32), grad_block.astype(jnp.float32))
        return ((key_sum, value_sum), grad_query_block)
    start = jnp.zeros((tokens, groups, HD), jnp.float32)
    (key_sum, value_sum), grad_query = lax.scan(backward_block, (start, start), (query_blocks, order_blocks, segment_blocks, grad_blocks, log_blocks, delta_blocks))
    grad_query = grad_query.reshape(tokens, QH * HD)
    grad_key = key_sum.reshape(tokens, KVH * HD).astype(jnp.bfloat16)
    grad_value = value_sum.reshape(tokens, KVH * HD).astype(jnp.bfloat16)
    return (output, grad_query, grad_key, grad_value)
```

```python
import functools
import math

import jax
import jax.numpy as jnp
from jax import lax
from jax.experimental import pallas as pl
from jax.experimental.pallas import tpu as pltpu
from jax.sharding import PartitionSpec as P

MESH = pl.DeviceIdType.MESH
NEG = -1e30
HD = 128
ROWS = 128
HEADS = 2
BF = jnp.bfloat16
F32 = jnp.float32
FACTORS = {64: (4, 16)}

NN = (((1,), (0,)), ((), ()))
NT = (((1,), (1,)), ((), ()))
TN = (((0,), (0,)), ((), ()))


def mm(a, b, dims):
    return lax.dot_general(a, b, dims, preferred_element_type=F32)


def at128(index):
    return pl.ds(pl.multiple_of(index * 128, 128), 128)


def at256(index):
    return pl.ds(pl.multiple_of(index * 256, 256), 256)


def kernel(
    nx, nz, ny, docs,
    q_hbm, k_hbm, v_hbm, w_hbm, g_hbm, order_hbm, segment_hbm,
    out_hbm, dq_hbm, dk_hbm, dv_hbm,
    q_own, w, order, segment, kbuf, vbuf, q_t, do_t, g_all,
    pos_row, pos_key, scores, probs, dscores, top, total, o_t, dq_t,
    stats, o_send, o_recv, factor, delta, fdo_t, fq_t,
    dk_part, dv_part, rs_send, rs_recv, dq_send, dq_recv,
    part_own, part_send, part_recv, y_send, y_recv,
    out_v, dq_v, dk_v, dv_v,
    in_sem, out_sem, kv_s, kv_r, q_s, q_r, do_s, do_r, st_s, st_r, o_s, o_r, dq_s, dq_r,
    gy_s, gy_r, gc_s, gc_r, pc_s, pc_r, py_s, py_r, rs_s, rs_r,
):
    context, tensor = lax.axis_index("context"), lax.axis_index("tensor")
    x, z = context // nz, lax.rem(context, nz)
    y, core = tensor // 2, lax.rem(tensor, 2)
    half = nz // 2
    exponent = math.log2(math.e) / math.sqrt(HD)
    scale = 1.0 / math.sqrt(HD)
    right = (x * nz + lax.rem(z + 1, nz), tensor)
    left = (x * nz + lax.rem(z + nz - 1, nz), tensor)
    x_at = [lax.rem(x + d, nx) for d in range(nx)]
    x_peer = [(x_at[d] * nz + z, tensor) for d in range(nx)]
    y_at = [lax.rem(y + d, ny) for d in range(ny)]
    y_peer = [(context, y_at[d] * 2 + core) for d in range(ny)]
    partner = (context, y * 2 + 1 - core)

    def remote(src, dst, send, recv, device):
        return pltpu.make_async_remote_copy(
            src_ref=src, dst_ref=dst, send_sem=send, recv_sem=recv, device_id=device, device_id_type=MESH
        )

    load_q = pltpu.make_async_copy(q_hbm, q_own, in_sem.at[0])
    load_order = pltpu.make_async_copy(order_hbm, order, in_sem.at[1])
    load_segment = pltpu.make_async_copy(segment_hbm, segment, in_sem.at[2])
    load_k = pltpu.make_async_copy(k_hbm, kbuf.at[at128(z)], in_sem.at[3])
    load_v = pltpu.make_async_copy(v_hbm, vbuf.at[at128(z)], in_sem.at[4])
    load_g = pltpu.make_async_copy(g_hbm, g_all.at[tensor], in_sem.at[5])
    load_w = pltpu.make_async_copy(w_hbm, w, in_sem.at[6])
    for load in (load_q, load_order, load_segment, load_k, load_v, load_g, load_w):
        load.start()

    barrier = pltpu.get_barrier_semaphore()
    peers = [right, left] + x_peer[1:] + y_peer[1:] + [partner]
    for peer in peers:
        pl.semaphore_signal(barrier, inc=1, device_id=peer, device_id_type=MESH)

    load_q.wait()
    for h in range(HEADS):
        q_t[:, at128(x * HEADS + h)] = q_own[:, h * HD : (h + 1) * HD].T

    pl.semaphore_wait(barrier, len(peers))

    def kv_copy(stream, step):
        buf = kbuf if stream < 2 else vbuf
        hop = step if stream % 2 == 0 else -step
        slot = buf.at[at128(lax.rem(z - hop + 2 * nz, nz))]
        return remote(slot, slot, kv_s.at[stream, step], kv_r.at[stream, step], right if stream % 2 == 0 else left)

    def kv_first(stream):
        src, buf = (k_hbm, kbuf) if stream < 2 else (v_hbm, vbuf)
        return remote(src, buf.at[at128(z)], kv_s.at[stream, 0], kv_r.at[stream, 0], right if stream % 2 == 0 else left)

    kv_steps = (half, half - 1, half - 1, half)

    def q_copy(d):
        slot = q_t.at[:, at256(x)]
        return remote(slot, slot, q_s.at[d], q_r.at[d], x_peer[d])

    def do_copy(d):
        slot = do_t.at[:, at256(x)]
        return remote(slot, slot, do_s.at[d], do_r.at[d], x_peer[d])

    def gy_copy(d):
        return remote(g_hbm, g_all.at[tensor], gy_s.at[d], gy_r.at[d], y_peer[d])

    def gc_copy(d):
        at = y_at[d] * 2 + core
        return remote(g_hbm if d == 0 else g_all.at[at], g_all.at[at], gc_s.at[d], gc_r.at[d], partner)

    for stream in (0, 1):
        if kv_steps[stream]:
            kv_first(stream).start()
    for d in range(1, nx):
        q_copy(d).start()
    for stream in (2, 3):
        if kv_steps[stream]:
            kv_first(stream).start()
    for d in range(1, ny):
        gy_copy(d).start()
    gc_copy(0).start()

    load_order.wait()
    load_segment.wait()
    starts = [
        jnp.sum(jnp.where(segment[...] < d, 1, 0), axis=(0, 1), keepdims=True) for d in range(1, docs)
    ]
    for xp in range(nx):
        own = order[pl.ds(xp * nz + z, 1), :]
        first = jnp.zeros_like(own)
        for start in starts:
            first = jnp.maximum(first, jnp.where(start <= own, start, 0))
        pos_row[xp : xp + 1, :] = own
        pos_row[nx + xp : nx + xp + 1, :] = first

    @pl.loop(0, nz)
    def _(b):
        row = order[pl.ds(x * nz + b, 1), :]
        pos_key[at128(b), :] = jnp.broadcast_to(row, (ROWS, 128)).T

    top[...] = jnp.full_like(top, NEG)
    load_k.wait()
    for d in range(1, nx):
        q_copy(d).wait_recv()

    def score_block(b):
        raw = mm(kbuf[at128(b), :], q_t[...], NN)
        key = pos_key[at128(b), :]
        for xp in range(nx):
            mask = (key >= pos_row[nx + xp : nx + xp + 1, :]) & (key <= pos_row[xp : xp + 1, :])
            for h in range(HEADS):
                lanes = slice((xp * HEADS + h) * 128, (xp * HEADS + h + 1) * 128)
                part = jnp.where(mask, raw[:, lanes], NEG)
                scores[at128(b), lanes] = part
                top[:, lanes] = jnp.maximum(top[:, lanes], jnp.max(part.reshape(ROWS // 8, 8, 128), axis=0))

    score_block(z)

    def cotangent():
        load_w.wait()
        load_g.wait()
        for d in range(ny):
            gc_copy(d).wait_recv()
        acc = jnp.zeros((HEADS * HD, ROWS), F32)
        features = g_hbm.shape[1]
        for t in range(2 * ny):
            acc = acc + mm(w[:, t * features : (t + 1) * features], g_all[t], NT)
        for h in range(HEADS):
            do_t[:, at128(x * HEADS + h)] = acc[h * HD : (h + 1) * HD, :].astype(BF)
        for d in range(1, nx):
            do_copy(d).start()

    def cotangent_relay():
        for d in range(1, ny):
            gy_copy(d).wait_recv()
        for d in range(1, ny):
            gc_copy(d).start()

    relay_at, cotangent_at = min(3, half - 1), min(4, half - 1)

    @pl.loop(0, half)
    def _(step):
        def arrive(stream):
            @pl.when(step < kv_steps[stream])
            def _():
                kv_copy(stream, step).wait_recv()

            @pl.when(step + 1 < kv_steps[stream])
            def _():
                kv_copy(stream, step + 1).start()

        arrive(0)
        arrive(1)
        score_block(lax.rem(z - 1 - step + nz, nz))
        arrive(2)
        arrive(3)

        @pl.when(step < half - 1)
        def _():
            score_block(lax.rem(z + 1 + step, nz))

        @pl.when(step == relay_at)
        def _():
            cotangent_relay()

        @pl.when(step == cotangent_at)
        def _():
            cotangent()

    load_v.wait()
    peak = jnp.max(top[...], axis=0, keepdims=True)
    total[...] = jnp.zeros_like(total)
    o_t[...] = jnp.zeros_like(o_t)
    keys = nz * ROWS
    chunk = min(512, keys)
    width = nx * HEADS * 128

    @pl.loop(0, keys // 128)
    def _(i):
        p = jnp.exp2((scores[at128(i), :] - peak) * exponent)
        probs[at128(i), :] = p.astype(BF)
        total[...] += jnp.sum(p.reshape(16, 8, width), axis=0)

    @pl.loop(0, keys // chunk)
    def _(i):
        at = pl.ds(pl.multiple_of(i * chunk, chunk), chunk)
        o_t[...] += mm(vbuf[at, :], probs[at, :], TN)

    for d in range(1, nx):
        do_copy(d).wait_recv()
    sums = jnp.sum(total[...], axis=0, keepdims=True)
    inner = jnp.sum(o_t[...] * do_t[...].astype(F32), axis=0, keepdims=True)
    slots = nx * HEADS
    for s in range(slots):
        lanes = slice(s * 128, (s + 1) * 128)
        stats[x, 0, s : s + 1, :] = peak[:, lanes]
        stats[x, 1, s : s + 1, :] = sums[:, lanes]
        stats[x, 2, s : s + 1, :] = inner[:, lanes]
    o_send[...] = o_t[...].astype(BF)

    def st_copy(d):
        return remote(stats.at[x], stats.at[x], st_s.at[d], st_r.at[d], x_peer[d])

    def o_copy(d):
        return remote(o_send.at[:, at256(x_at[d])], o_recv.at[d], o_s.at[d], o_r.at[d], x_peer[d])

    for d in range(1, nx):
        st_copy(d).start()
    for d in range(1, nx):
        o_copy(d).start()
    for d in range(1, nx):
        st_copy(d).wait_recv()

    peak_all = functools.reduce(jnp.maximum, [stats[i, 0] for i in range(nx)])
    weight = [jnp.exp2((stats[i, 0] - peak_all) * exponent) for i in range(nx)]
    inverse = 1.0 / functools.reduce(jnp.add, [weight[i] * stats[i, 1] for i in range(nx)])
    delta[...] = inverse * functools.reduce(jnp.add, [weight[i] * stats[i, 2] for i in range(nx)])
    for i in range(nx):
        factor[i] = weight[i] * inverse
    mine = factor[x]
    for s in range(slots):
        lanes = slice(s * 128, (s + 1) * 128)
        f = mine[s : s + 1, :]
        fdo_t[:, lanes] = (do_t[:, lanes].astype(F32) * f).astype(BF)
        fq_t[:, lanes] = (q_t[:, lanes].astype(F32) * (f * scale)).astype(BF)

    dq_t[...] = jnp.zeros_like(dq_t)

    def grad_block(b):
        p = probs[at128(b), :]
        dp = mm(vbuf[at128(b), :], do_t[...], NN)
        for s in range(slots):
            lanes = slice(s * 128, (s + 1) * 128)
            dscores[at128(b), lanes] = (p[:, lanes].astype(F32) * (dp[:, lanes] - delta[s : s + 1, :])).astype(BF)
        ds = dscores[at128(b), :]
        dv_part[b] = mm(p, fdo_t[...], NT)
        dk_part[b] = mm(ds, fq_t[...], NT)
        dq_t[...] += mm(kbuf[at128(b), :], ds, TN)

    def rs_copy(stream, step):
        return remote(
            rs_send.at[stream, step], rs_recv.at[stream, step], rs_s.at[stream, step], rs_r.at[stream, step],
            right if stream % 2 == 0 else left,
        )

    rs_from = (0, 1, 1, 0)

    def rs_step(stream, step):
        hop = half - step
        owner = lax.rem(z + (hop if stream % 2 == 0 else nz - hop), nz)
        part = dk_part if stream < 2 else dv_part

        @pl.when(step == rs_from[stream])
        def _():
            rs_send[stream, step] = part[owner].astype(BF)
            rs_copy(stream, step).start()

        @pl.when(step > rs_from[stream])
        def _():
            rs_copy(stream, step - 1).wait_recv()
            rs_send[stream, step] = (part[owner] + rs_recv[stream, step - 1].astype(F32)).astype(BF)
            rs_copy(stream, step).start()

    def dq_copy(d):
        return remote(dq_send.at[:, at256(x_at[d])], dq_recv.at[d], dq_s.at[d], dq_r.at[d], x_peer[d])

    def pc_copy():
        return remote(part_send, part_recv, pc_s.at[0], pc_r.at[0], partner)

    def py_copy(d):
        return remote(y_send.at[y_at[d]], y_recv.at[d], py_s.at[d], py_r.at[d], y_peer[d])

    features = g_hbm.shape[1]

    def project():
        for d in range(1, nx):
            o_copy(d).wait_recv()
        attended = []
        for h in range(HEADS):
            acc = o_send[:, at128(x * HEADS + h)].astype(F32) * factor[x, pl.ds(x * HEADS + h, 1), :]
            for d in range(1, nx):
                source = lax.rem(x - d + nx, nx)
                acc = acc + (
                    o_recv[d, :, h * 128 : (h + 1) * 128].astype(F32) * factor[source, pl.ds(x * HEADS + h, 1), :]
                )
            attended.append(acc.astype(BF))
        attended = jnp.concatenate(attended, axis=0)

        @pl.loop(0, ny)
        def _(yp):
            for c in range(2):
                at = pl.ds(pl.multiple_of((yp * 2 + c) * features, features), features)
                part = mm(attended, w[:, at], TN)

                @pl.when(core == c)
                def _():
                    part_own[yp] = part

                @pl.when(core != c)
                def _():
                    part_send[yp] = part.astype(BF)

        pc_copy().start()

    def spread():
        pc_copy().wait_recv()

        @pl.loop(0, ny)
        def _(yp):
            part = part_own[yp] + part_recv[yp].astype(F32)
            part_own[yp] = part
            y_send[yp] = part.astype(BF)

        for d in range(1, ny):
            py_copy(d).start()

    def send_dq():
        for s in range(slots):
            lanes = slice(s * 128, (s + 1) * 128)
            dq_t[:, lanes] = dq_t[:, lanes] * (factor[x, s : s + 1, :] * scale)
        dq_send[...] = dq_t[...].astype(BF)
        for d in range(1, nx):
            dq_copy(d).start()

    ahead = half // 2
    project_at, spread_at = min(1, half - 1), min(3, half - 1)
    grad_block(lax.rem(z + half, nz))

    @pl.loop(0, half)
    def _(step):
        for stream in (3, 0, 1, 2):
            rs_step(stream, step)

        @pl.when(step < max(1, ahead))
        def _():
            for later in range(2 if ahead else 1):
                hop = half - ((2 if ahead else 1) * step + 1 + later)
                grad_block(lax.rem(z + hop + nz, nz))

                @pl.when(hop > 0)
                def _():
                    grad_block(lax.rem(z - hop + nz, nz))

        @pl.when(step == max(1, ahead) - 1)
        def _():
            send_dq()

        @pl.when(step == project_at)
        def _():
            project()

        @pl.when(step == spread_at)
        def _():
            spread()

    for d in range(1, ny):
        py_copy(d).wait_recv()
    out = part_own[y]
    for d in range(1, ny):
        out = out + y_recv[d].astype(F32)
    out_v[...] = out.astype(BF)
    store_out = pltpu.make_async_copy(out_v, out_hbm, out_sem.at[0])
    store_out.start()

    for d in range(1, nx):
        dq_copy(d).wait_recv()
    for h in range(HEADS):
        acc = dq_t[:, at128(x * HEADS + h)]
        for d in range(1, nx):
            acc = acc + dq_recv[d, :, h * 128 : (h + 1) * 128].astype(F32)
        dq_v[:, h * 128 : (h + 1) * 128] = acc.T.astype(BF)
    store_dq = pltpu.make_async_copy(dq_v, dq_hbm, out_sem.at[1])
    store_dq.start()

    def owned(part, streams):
        acc = part[z]
        for stream in streams:
            if half > rs_from[stream]:
                rs_copy(stream, half - 1).wait_recv()
                acc = acc + rs_recv[stream, half - 1].astype(F32)
        return acc.astype(BF)

    dv_v[...] = owned(dv_part, (2, 3))
    store_dv = pltpu.make_async_copy(dv_v, dv_hbm, out_sem.at[2])
    store_dv.start()
    dk_v[...] = owned(dk_part, (0, 1))
    store_dk = pltpu.make_async_copy(dk_v, dk_hbm, out_sem.at[3])
    store_dk.start()

    for stream in range(4):
        for step in range(half):
            if step < kv_steps[stream]:
                (kv_first(stream) if step == 0 else kv_copy(stream, step)).wait_send()
            if step >= rs_from[stream]:
                rs_copy(stream, step).wait_send()
    for d in range(1, nx):
        for copy in (q_copy, do_copy, st_copy, o_copy, dq_copy):
            copy(d).wait_send()
    for d in range(1, ny):
        gy_copy(d).wait_send()
        py_copy(d).wait_send()
    for d in range(ny):
        gc_copy(d).wait_send()
    pc_copy().wait_send()
    for store in (store_out, store_dq, store_dv, store_dk):
        store.wait()


def per_device(nx, nz, ny, docs, query, key_proj, value, out_weight, grad_out, order, segment):
    features = grad_out.shape[1]
    half = nz // 2
    keys, width, slots = nz * ROWS, nx * HEADS * 128, nx * HEADS
    tokens = order.shape[0]
    order = order.reshape(tokens // 128, 128)
    segment = segment.reshape(tokens // 128, 128)

    def vm(*shape, dtype=BF):
        return pltpu.VMEM(shape, dtype)

    def sem(*shape):
        return pltpu.SemaphoreType.DMA(shape)

    scratch = [
        vm(ROWS, HEADS * HD), vm(HEADS * HD, out_weight.shape[1]),
        vm(tokens // 128, 128, dtype=jnp.int32), vm(tokens // 128, 128, dtype=jnp.int32),
        vm(keys, HD), vm(keys, HD), vm(HD, width), vm(HD, width), vm(2 * ny, ROWS, features),
        vm(2 * nx, 128, dtype=jnp.int32), vm(keys, 128, dtype=jnp.int32),
        vm(keys, width, dtype=F32), vm(keys, width), vm(keys, width),
        vm(8, width, dtype=F32), vm(8, width, dtype=F32), vm(HD, width, dtype=F32), vm(HD, width, dtype=F32),
        vm(nx, 3, slots, 128, dtype=F32), vm(HD, width), vm(nx, HD, 256),
        vm(nx, slots, 128, dtype=F32), vm(slots, 128, dtype=F32), vm(HD, width), vm(HD, width),
        vm(nz, ROWS, HD, dtype=F32), vm(nz, ROWS, HD, dtype=F32),
        vm(4, half, ROWS, HD), vm(4, half, ROWS, HD), vm(HD, width), vm(nx, HD, 256),
        vm(ny, ROWS, features, dtype=F32), vm(ny, ROWS, features), vm(ny, ROWS, features),
        vm(ny, ROWS, features), vm(ny, ROWS, features),
        vm(ROWS, features), vm(ROWS, HEADS * HD), vm(ROWS, HD), vm(ROWS, HD),
        sem(7), sem(4), sem(4, half), sem(4, half),
    ] + [sem(nx)] * 10 + [sem(ny)] * 4 + [sem(1)] * 2 + [sem(ny)] * 2 + [sem(4, half)] * 2
    flops = 2 * width * keys * HD * 6 + 4 * ROWS * HEADS * HD * out_weight.shape[1]
    return pl.pallas_call(
        functools.partial(kernel, nx, nz, ny, docs),
        out_shape=[
            jax.ShapeDtypeStruct((ROWS, features), BF),
            jax.ShapeDtypeStruct((ROWS, HEADS * HD), BF),
            jax.ShapeDtypeStruct((ROWS, HD), BF),
            jax.ShapeDtypeStruct((ROWS, HD), BF),
        ],
        in_specs=[pl.BlockSpec(memory_space=pl.ANY)] * 7,
        out_specs=[pl.BlockSpec(memory_space=pl.ANY)] * 4,
        scratch_shapes=scratch,
        compiler_params=pltpu.CompilerParams(
            collective_id=0, has_side_effects=True, vmem_limit_bytes=48 * 1024 * 1024
        ),
        cost_estimate=pl.CostEstimate(flops=flops, bytes_accessed=4 << 20, transcendentals=keys * width),
    )(query, key_proj, value, out_weight, grad_out, order, segment)


def solution(mesh):
    nx, nz = FACTORS[mesh.shape["context"]]
    ny = mesh.shape["tensor"] // 2
    return jax.shard_map(
        functools.partial(per_device, nx, nz, ny, 8),
        mesh=mesh,
        in_specs=(
            P("context", "tensor"),
            P("context", "tensor"),
            P("context", "tensor"),
            P("tensor", None),
            P("context", "tensor"),
            P(),
            P(),
        ),
        out_specs=(P("context", "tensor"),) * 4,
        check_vma=False,
    )
```

```python
import functools
import math

import jax
import jax.numpy as jnp
from jax import lax
from jax.experimental import pallas as pl
from jax.experimental.pallas import tpu as pltpu
from jax.sharding import PartitionSpec as P

MESH = pl.DeviceIdType.MESH
NEG = -1e30
HD = 128
ROWS = 128
HEADS = 2
BF = jnp.bfloat16
F32 = jnp.float32
FACTORS = {64: (4, 16)}
PARENT = {3: 0, 1: 0, 6: 3, 2: 3, 4: 3, 5: 6, 7: 6, 8: 6}
LEAVES = (1, 2, 4, 5, 7, 8)
SIGNS = {(False, 0): (1, -1), (False, 1): (1, -1), (True, 0): (1,), (True, 1): (-1,)}

NN = (((1,), (0,)), ((), ()))
NT = (((1,), (1,)), ((), ()))
TN = (((0,), (0,)), ((), ()))


def mm(a, b, dims):
    return lax.dot_general(a, b, dims, preferred_element_type=F32)


def at128(index):
    return pl.ds(pl.multiple_of(index * 128, 128), 128)


def at256(index):
    return pl.ds(pl.multiple_of(index * 256, 256), 256)


def kernel(
    nx, nz, ny, docs,
    q_hbm, k_hbm, v_hbm, w_hbm, g_hbm, order_hbm, segment_hbm,
    out_hbm, dq_hbm, dk_hbm, dv_hbm,
    q_own, w, order, segment, kbuf, vbuf, q_t, do_t, g_all,
    pos_row, pos_key, scores, probs, dscores, top, total, o_t, dq_t,
    stats, inners, o_send, o_recv, factor, delta, fdo_t, fq_t,
    dk_part, dv_part, rs_send, rs_recv, dq_send, dq_recv,
    part_own, part_send, part_recv, y_send, y_recv,
    out_v, dq_v, dk_v, dv_v,
    in_sem, out_sem, kv_s, kv_r, q_s, q_r, do_s, do_r, st_s, st_r, in_s, in_r, o_s, o_r, dq_s, dq_r,
    gy_s, gy_r, gc_s, gc_r, pc_s, pc_r, py_s, py_r, rs_s, rs_r,
):
    context, tensor = lax.axis_index("context"), lax.axis_index("tensor")
    x, z = context // nz, lax.rem(context, nz)
    y, core = tensor // 2, lax.rem(tensor, 2)
    exponent = math.log2(math.e) / math.sqrt(HD)
    scale = 1.0 / math.sqrt(HD)
    slots = nx * HEADS
    width = slots * 128
    keys = nz * ROWS
    features = g_hbm.shape[1]
    x_at = [lax.rem(x + d, nx) for d in range(nx)]
    x_peer = [(x_at[d] * nz + z, tensor) for d in range(nx)]
    y_at = [lax.rem(y + d, ny) for d in range(ny)]
    y_peer = [(context, y_at[d] * 2 + core) for d in range(ny)]
    partner = (context, y * 2 + 1 - core)

    def z_at(offset):
        return lax.rem(z + offset + 2 * nz, nz)

    def z_peer(offset):
        return (x * nz + z_at(offset), tensor)

    def remote(src, dst, send, recv, device):
        return pltpu.make_async_remote_copy(
            src_ref=src, dst_ref=dst, send_sem=send, recv_sem=recv, device_id=device, device_id_type=MESH
        )

    load_q = pltpu.make_async_copy(q_hbm, q_own, in_sem.at[0])
    load_order = pltpu.make_async_copy(order_hbm, order, in_sem.at[1])
    load_segment = pltpu.make_async_copy(segment_hbm, segment, in_sem.at[2])
    load_k = pltpu.make_async_copy(k_hbm, kbuf.at[at128(z)], in_sem.at[3])
    load_v = pltpu.make_async_copy(v_hbm, vbuf.at[at128(z)], in_sem.at[4])
    load_g = pltpu.make_async_copy(g_hbm, g_all.at[tensor], in_sem.at[5])
    load_w = pltpu.make_async_copy(w_hbm, w, in_sem.at[6])

    barrier = pltpu.get_barrier_semaphore()
    peers = [z_peer(d) for d in (1, -1, 2, -2, 3, -3)] + x_peer[1:] + y_peer[1:] + [partner]
    for peer in peers:
        pl.semaphore_signal(barrier, inc=1, device_id=peer, device_id_type=MESH)
    for load in (load_q, load_order, load_segment, load_k, load_v, load_g, load_w):
        load.start()

    load_q.wait()
    for h in range(HEADS):
        q_t[:, at128(x * HEADS + h)] = q_own[:, h * HD : (h + 1) * HD].T

    pl.semaphore_wait(barrier, len(peers))

    def kv_copy(stream, sign, far):
        near = PARENT[far]
        src, buf = ((k_hbm, kbuf), (v_hbm, vbuf))[stream]
        slot = buf.at[at128(z_at(-sign * near))]
        at = sign * far + 8
        return remote(src if near == 0 else slot, slot, kv_s.at[stream, at], kv_r.at[stream, at], z_peer(sign * (far - near)))

    def kv_start(stream, *fars):
        for far in fars:
            for sign in SIGNS[far == 8, stream]:
                kv_copy(stream, sign, far).start()

    def kv_wait(stream, *fars):
        for far in fars:
            for sign in SIGNS[far == 8, stream]:
                kv_copy(stream, sign, far).wait_recv()

    def both(fn):
        @pl.loop(0, 2)
        def _(j):
            fn(1 - 2 * j)

    def q_copy(d):
        slot = q_t.at[:, at256(x)]
        return remote(slot, slot, q_s.at[d], q_r.at[d], x_peer[d])

    def do_copy(d):
        slot = do_t.at[:, at256(x)]
        return remote(slot, slot, do_s.at[d], do_r.at[d], x_peer[d])

    def gy_copy(d):
        return remote(g_hbm, g_all.at[tensor], gy_s.at[d], gy_r.at[d], y_peer[d])

    def gc_copy(d):
        at = y_at[d] * 2 + core
        return remote(g_hbm if d == 0 else g_all.at[at], g_all.at[at], gc_s.at[d], gc_r.at[d], partner)

    kv_start(0, 3, 1)
    for d in range(1, nx):
        q_copy(d).start()
    for d in range(1, ny):
        gy_copy(d).start()
    gc_copy(0).start()
    kv_start(1, 3, 1)

    load_order.wait()
    load_segment.wait()
    starts = [
        jnp.sum(jnp.where(segment[...] < d, 1, 0), axis=(0, 1), keepdims=True) for d in range(1, docs)
    ]
    for xp in range(nx):
        own = order[pl.ds(xp * nz + z, 1), :]
        first = jnp.zeros_like(own)
        for start in starts:
            first = jnp.maximum(first, jnp.where(start <= own, start, 0))
        pos_row[xp : xp + 1, :] = own
        pos_row[nx + xp : nx + xp + 1, :] = first

    @pl.loop(0, nz)
    def _(b):
        row = order[pl.ds(x * nz + b, 1), :]
        pos_key[at128(b), :] = jnp.broadcast_to(row, (ROWS, 128)).T

    top[...] = jnp.full_like(top, NEG)

    def score_block(b):
        raw = mm(kbuf[at128(b), :], q_t[...], NN)
        key = pos_key[at128(b), :]
        for xp in range(nx):
            mask = (key >= pos_row[nx + xp : nx + xp + 1, :]) & (key <= pos_row[xp : xp + 1, :])
            for h in range(HEADS):
                lanes = slice((xp * HEADS + h) * 128, (xp * HEADS + h + 1) * 128)
                part = jnp.where(mask, raw[:, lanes], NEG)
                scores[at128(b), lanes] = part
                top[:, lanes] = jnp.maximum(top[:, lanes], jnp.max(part.reshape(ROWS // 8, 8, 128), axis=0))

    def score_far(*fars, wait=True):
        def one(sign):
            for far in fars:
                if wait:
                    kv_copy(0, sign, far).wait_recv()
                score_block(z_at(-sign * far))

        both(one)

    def cotangent_relay():
        for d in range(1, ny):
            gy_copy(d).wait_recv()
        for d in range(1, ny):
            gc_copy(d).start()

    def cotangent():
        load_w.wait()
        load_g.wait()
        for d in range(ny):
            gc_copy(d).wait_recv()
        acc = jnp.zeros((HEADS * HD, ROWS), F32)
        for t in range(2 * ny):
            acc = acc + mm(w[:, t * features : (t + 1) * features], g_all[t], NT)
        for h in range(HEADS):
            do_t[:, at128(x * HEADS + h)] = acc[h * HD : (h + 1) * HD, :].astype(BF)
        for d in range(1, nx):
            do_copy(d).start()

    kv_wait(0, 3)
    kv_start(0, 6, 2, 4)
    load_k.wait()
    for d in range(1, nx):
        q_copy(d).wait_recv()
    score_block(z)
    score_far(3, wait=False)
    kv_wait(1, 3)
    kv_start(1, 6, 2, 4)
    score_far(1)
    kv_wait(0, 6)
    kv_start(0, 5, 7, 8)
    cotangent_relay()
    score_far(6, wait=False)
    score_far(2, 4)
    kv_wait(1, 6)
    kv_start(1, 5, 7, 8)
    cotangent()
    score_far(5, 7)
    kv_wait(0, 8)
    score_block(z_at(-8))

    peak = jnp.max(top[...], axis=0, keepdims=True)
    total[...] = jnp.zeros_like(total)

    @pl.loop(0, nz)
    def _(i):
        p = jnp.exp2((scores[at128(i), :] - peak) * exponent)
        probs[at128(i), :] = p.astype(BF)
        total[...] += jnp.sum(p.reshape(16, 8, width), axis=0)

    sums = jnp.sum(total[...], axis=0, keepdims=True)
    for s in range(slots):
        lanes = slice(s * 128, (s + 1) * 128)
        stats[x, 0, s : s + 1, :] = peak[:, lanes]
        stats[x, 1, s : s + 1, :] = sums[:, lanes]

    def st_copy(d):
        return remote(stats.at[x], stats.at[x], st_s.at[d], st_r.at[d], x_peer[d])

    def in_copy(d):
        return remote(inners.at[x], inners.at[x], in_s.at[d], in_r.at[d], x_peer[d])

    def o_copy(d):
        return remote(o_send.at[:, at256(x_at[d])], o_recv.at[d], o_s.at[d], o_r.at[d], x_peer[d])

    for d in range(1, nx):
        st_copy(d).start()
    for d in range(1, nx):
        do_copy(d).wait_recv()
    for d in range(1, nx):
        st_copy(d).wait_recv()

    peak_all = functools.reduce(jnp.maximum, [stats[i, 0] for i in range(nx)])
    weight = [jnp.exp2((stats[i, 0] - peak_all) * exponent) for i in range(nx)]
    inverse = 1.0 / functools.reduce(jnp.add, [weight[i] * stats[i, 1] for i in range(nx)])
    for i in range(nx):
        factor[i] = weight[i] * inverse
    mine = factor[x]
    for s in range(slots):
        lanes = slice(s * 128, (s + 1) * 128)
        f = mine[s : s + 1, :]
        fdo_t[:, lanes] = (do_t[:, lanes].astype(F32) * f).astype(BF)
        fq_t[:, lanes] = (q_t[:, lanes].astype(F32) * (f * scale)).astype(BF)

    def rs_copy(stream, sign, far):
        at = sign * far + 8
        return remote(
            rs_send.at[stream, at], rs_recv.at[stream, at], rs_s.at[stream, at], rs_r.at[stream, at],
            z_peer(sign * (PARENT[far] - far)),
        )

    def rs_out(stream, sign, far, *kids):
        acc = (dk_part, dv_part)[stream][z_at(-sign * far)]
        for kid in kids:
            rs_copy(stream, sign, kid).wait_recv()
            acc = acc + rs_recv[stream, sign * kid + 8].astype(F32)
        rs_send[stream, sign * far + 8] = acc.astype(BF)
        rs_copy(stream, sign, far).start()

    def rs_hubs(stream, far):
        for sign in (1, -1):
            kids = (2, 4, 6) if far == 3 else (5, 7, 8) if sign in SIGNS[True, stream] else (5, 7)
            rs_out(stream, sign, far, *kids)

    def dv_block(b):
        dv_part[b] = mm(probs[at128(b), :], fdo_t[...], NT)

    def ds_block(b):
        dp = mm(vbuf[at128(b), :], do_t[...], NN)
        for s in range(slots):
            lanes = slice(s * 128, (s + 1) * 128)
            p = probs[at128(b), lanes].astype(F32)
            dscores[at128(b), lanes] = (p * (dp[:, lanes] - delta[s : s + 1, :])).astype(BF)
        ds = dscores[at128(b), :]
        dk_part[b] = mm(ds, fq_t[...], NT)
        dq_t[...] += mm(kbuf[at128(b), :], ds, TN)

    def grad_far(stream, *fars):
        block = (ds_block, dv_block)[stream]

        def one(sign):
            for far in fars:
                block(z_at(-sign * far))
                if far in LEAVES:
                    rs_out(stream, sign, far)

        both(one)

    def grad_antipode(stream):
        (ds_block, dv_block)[stream](z_at(-8))
        rs_out(stream, SIGNS[True, stream][0], 8)

    grad_far(1, 5, 7)
    grad_antipode(1)
    grad_far(1, 2, 4)
    grad_far(1, 1, 6, 3)
    dv_block(z)

    load_v.wait()
    kv_wait(1, 1, 2, 4, 5, 7, 8)
    o_t[...] = jnp.zeros_like(o_t)
    chunk = min(512, keys)

    @pl.loop(0, keys // chunk)
    def _(i):
        at = pl.ds(pl.multiple_of(i * chunk, chunk), chunk)
        o_t[...] += mm(vbuf[at, :], probs[at, :], TN)

    inner = jnp.sum(o_t[...] * do_t[...].astype(F32), axis=0, keepdims=True)
    for s in range(slots):
        inners[x, s : s + 1, :] = inner[:, s * 128 : (s + 1) * 128]
    for d in range(1, nx):
        in_copy(d).start()
    o_send[...] = o_t[...].astype(BF)
    for d in range(1, nx):
        o_copy(d).start()
    rs_hubs(1, 6)
    dq_t[...] = jnp.zeros_like(dq_t)
    for d in range(1, nx):
        in_copy(d).wait_recv()
    delta[...] = functools.reduce(jnp.add, [factor[i] * inners[i] for i in range(nx)])

    def dq_copy(d):
        return remote(dq_send.at[:, at256(x_at[d])], dq_recv.at[d], dq_s.at[d], dq_r.at[d], x_peer[d])

    def pc_copy():
        return remote(part_send, part_recv, pc_s.at[0], pc_r.at[0], partner)

    def py_copy(d):
        return remote(y_send.at[y_at[d]], y_recv.at[d], py_s.at[d], py_r.at[d], y_peer[d])

    def project():
        for d in range(1, nx):
            o_copy(d).wait_recv()
        attended = []
        for h in range(HEADS):
            acc = o_send[:, at128(x * HEADS + h)].astype(F32) * factor[x, pl.ds(x * HEADS + h, 1), :]
            for d in range(1, nx):
                source = lax.rem(x - d + nx, nx)
                acc = acc + (
                    o_recv[d, :, h * 128 : (h + 1) * 128].astype(F32) * factor[source, pl.ds(x * HEADS + h, 1), :]
                )
            attended.append(acc.astype(BF))
        attended = jnp.concatenate(attended, axis=0)

        @pl.loop(0, ny)
        def _(yp):
            for c in range(2):
                at = pl.ds(pl.multiple_of((yp * 2 + c) * features, features), features)
                part = mm(attended, w[:, at], TN)

                @pl.when(core == c)
                def _():
                    part_own[yp] = part

                @pl.when(core != c)
                def _():
                    part_send[yp] = part.astype(BF)

        pc_copy().start()

    def spread():
        pc_copy().wait_recv()

        @pl.loop(0, ny)
        def _(yp):
            part = part_own[yp] + part_recv[yp].astype(F32)
            part_own[yp] = part
            y_send[yp] = part.astype(BF)

        for d in range(1, ny):
            py_copy(d).start()

    def send_dq():
        for s in range(slots):
            lanes = slice(s * 128, (s + 1) * 128)
            dq_t[:, lanes] = dq_t[:, lanes] * (factor[x, s : s + 1, :] * scale)
        dq_send[...] = dq_t[...].astype(BF)
        for d in range(1, nx):
            dq_copy(d).start()

    grad_far(0, 5, 7)
    grad_antipode(0)
    grad_far(0, 2, 4)
    rs_hubs(1, 3)
    project()
    grad_far(0, 1, 6, 3)
    ds_block(z)
    rs_hubs(0, 6)
    spread()
    send_dq()
    rs_hubs(0, 3)

    def owned(part, stream):
        acc = part[z]
        for far in (1, 3):
            for sign in (1, -1):
                rs_copy(stream, sign, far).wait_recv()
                acc = acc + rs_recv[stream, sign * far + 8].astype(F32)
        return acc.astype(BF)

    dv_v[...] = owned(dv_part, 1)
    store_dv = pltpu.make_async_copy(dv_v, dv_hbm, out_sem.at[2])
    store_dv.start()
    for d in range(1, nx):
        dq_copy(d).wait_recv()
    for h in range(HEADS):
        acc = dq_t[:, at128(x * HEADS + h)]
        for d in range(1, nx):
            acc = acc + dq_recv[d, :, h * 128 : (h + 1) * 128].astype(F32)
        dq_v[:, h * 128 : (h + 1) * 128] = acc.T.astype(BF)
    store_dq = pltpu.make_async_copy(dq_v, dq_hbm, out_sem.at[1])
    store_dq.start()
    for d in range(1, ny):
        py_copy(d).wait_recv()
    out = part_own[y]
    for d in range(1, ny):
        out = out + y_recv[d].astype(F32)
    out_v[...] = out.astype(BF)
    store_out = pltpu.make_async_copy(out_v, out_hbm, out_sem.at[0])
    store_out.start()
    dk_v[...] = owned(dk_part, 0)
    store_dk = pltpu.make_async_copy(dk_v, dk_hbm, out_sem.at[3])
    store_dk.start()

    for stream in range(2):
        for far in PARENT:
            for sign in SIGNS[far == 8, stream]:
                kv_copy(stream, sign, far).wait_send()
                rs_copy(stream, sign, far).wait_send()
    for d in range(1, nx):
        for copy in (q_copy, do_copy, st_copy, in_copy, o_copy, dq_copy):
            copy(d).wait_send()
    for d in range(1, ny):
        gy_copy(d).wait_send()
        py_copy(d).wait_send()
    for d in range(ny):
        gc_copy(d).wait_send()
    pc_copy().wait_send()
    for store in (store_out, store_dq, store_dv, store_dk):
        store.wait()


def per_device(nx, nz, ny, docs, query, key_proj, value, out_weight, grad_out, order, segment):
    features = grad_out.shape[1]
    keys, width, slots = nz * ROWS, nx * HEADS * 128, nx * HEADS
    tokens = order.shape[0]
    order = order.reshape(tokens // 128, 128)
    segment = segment.reshape(tokens // 128, 128)

    def vm(*shape, dtype=BF):
        return pltpu.VMEM(shape, dtype)

    def sem(*shape):
        return pltpu.SemaphoreType.DMA(shape)

    scratch = [
        vm(ROWS, HEADS * HD), vm(HEADS * HD, out_weight.shape[1]),
        vm(tokens // 128, 128, dtype=jnp.int32), vm(tokens // 128, 128, dtype=jnp.int32),
        vm(keys, HD), vm(keys, HD), vm(HD, width), vm(HD, width), vm(2 * ny, ROWS, features),
        vm(2 * nx, 128, dtype=jnp.int32), vm(keys, 128, dtype=jnp.int32),
        vm(keys, width, dtype=F32), vm(keys, width), vm(keys, width),
        vm(8, width, dtype=F32), vm(8, width, dtype=F32), vm(HD, width, dtype=F32), vm(HD, width, dtype=F32),
        vm(nx, 2, slots, 128, dtype=F32), vm(nx, slots, 128, dtype=F32), vm(HD, width), vm(nx, HD, 256),
        vm(nx, slots, 128, dtype=F32), vm(slots, 128, dtype=F32), vm(HD, width), vm(HD, width),
        vm(nz, ROWS, HD, dtype=F32), vm(nz, ROWS, HD, dtype=F32),
        vm(2, 17, ROWS, HD), vm(2, 17, ROWS, HD), vm(HD, width), vm(nx, HD, 256),
        vm(ny, ROWS, features, dtype=F32), vm(ny, ROWS, features), vm(ny, ROWS, features),
        vm(ny, ROWS, features), vm(ny, ROWS, features),
        vm(ROWS, features), vm(ROWS, HEADS * HD), vm(ROWS, HD), vm(ROWS, HD),
        sem(7), sem(4), sem(2, 17), sem(2, 17),
    ] + [sem(nx)] * 12 + [sem(ny)] * 4 + [sem(1)] * 2 + [sem(ny)] * 2 + [sem(2, 17)] * 2
    flops = 2 * width * keys * HD * 6 + 4 * ROWS * HEADS * HD * out_weight.shape[1]
    return pl.pallas_call(
        functools.partial(kernel, nx, nz, ny, docs),
        out_shape=[
            jax.ShapeDtypeStruct((ROWS, features), BF),
            jax.ShapeDtypeStruct((ROWS, HEADS * HD), BF),
            jax.ShapeDtypeStruct((ROWS, HD), BF),
            jax.ShapeDtypeStruct((ROWS, HD), BF),
        ],
        in_specs=[pl.BlockSpec(memory_space=pl.ANY)] * 7,
        out_specs=[pl.BlockSpec(memory_space=pl.ANY)] * 4,
        scratch_shapes=scratch,
        compiler_params=pltpu.CompilerParams(
            collective_id=0, has_side_effects=True, vmem_limit_bytes=60 * 1024 * 1024
        ),
        cost_estimate=pl.CostEstimate(flops=flops, bytes_accessed=4 << 20, transcendentals=keys * width),
    )(query, key_proj, value, out_weight, grad_out, order, segment)


def solution(mesh):
    nx, nz = FACTORS[mesh.shape["context"]]
    ny = mesh.shape["tensor"] // 2
    return jax.shard_map(
        functools.partial(per_device, nx, nz, ny, 8),
        mesh=mesh,
        in_specs=(
            P("context", "tensor"),
            P("context", "tensor"),
            P("context", "tensor"),
            P("tensor", None),
            P("context", "tensor"),
            P(),
            P(),
        ),
        out_specs=(P("context", "tensor"),) * 4,
        check_vma=False,
    )
```

```python
import functools
import math

import jax
import jax.numpy as jnp
from jax import lax
from jax.experimental import pallas as pl
from jax.experimental.pallas import tpu as pltpu
from jax.sharding import PartitionSpec as P

MESH = pl.DeviceIdType.MESH
NEG = -1e30
HD = 128
ROWS = 128
HEADS = 2
BF = jnp.bfloat16
F32 = jnp.float32
FACTORS = {64: (4, 16)}
PARENT = {3: 0, 1: 0, 6: 3, 2: 3, 4: 3, 5: 6, 7: 6, 8: 6}
UP = (PARENT, PARENT)
LEAVES = (1, 2, 4, 5, 7, 8)
SIGNS = {(False, 0): (1, -1), (False, 1): (1, -1), (True, 0): (1,), (True, 1): (-1,)}

NN = (((1,), (0,)), ((), ()))
NT = (((1,), (1,)), ((), ()))
TN = (((0,), (0,)), ((), ()))


def mm(a, b, dims):
    return lax.dot_general(a, b, dims, preferred_element_type=F32)


def at128(index):
    return pl.ds(pl.multiple_of(index * 128, 128), 128)


def at256(index):
    return pl.ds(pl.multiple_of(index * 256, 256), 256)


def kernel(
    nx, nz, ny, docs,
    q_hbm, k_hbm, v_hbm, w_hbm, g_hbm, order_hbm, segment_hbm,
    out_v, dq_v, dk_v, dv_v,
    q_own, w, order, segment, kbuf, vbuf, q_t, do_t, g_all,
    pos_row, pos_key, scores, probs, dscores, top, total, o_t, dq_t,
    stats, inners, o_send, o_recv, factor, delta, fdo_t, fq_t,
    dk_part, dv_part, rs_send, rs_recv, dq_send, dq_recv,
    part_own, part_send, part_recv, y_send, y_recv,
    in_sem, kv_s, kv_r, q_s, q_r, do_s, do_r, st_s, st_r, in_s, in_r, o_s, o_r, dq_s, dq_r,
    gy_s, gy_r, gc_s, gc_r, pc_s, pc_r, py_s, py_r, rs_s, rs_r,
):
    context, tensor = lax.axis_index("context"), lax.axis_index("tensor")
    x, z = context // nz, lax.rem(context, nz)
    y, core = tensor // 2, lax.rem(tensor, 2)
    exponent = math.log2(math.e) / math.sqrt(HD)
    scale = 1.0 / math.sqrt(HD)
    slots = nx * HEADS
    width = slots * 128
    keys = nz * ROWS
    features = g_hbm.shape[1]
    x_at = [lax.rem(x + d, nx) for d in range(nx)]
    x_peer = [(x_at[d] * nz + z, tensor) for d in range(nx)]
    y_at = [lax.rem(y + d, ny) for d in range(ny)]
    y_peer = [(context, y_at[d] * 2 + core) for d in range(ny)]
    partner = (context, y * 2 + 1 - core)

    def z_at(offset):
        return lax.rem(z + offset + 2 * nz, nz)

    def z_peer(offset):
        return (x * nz + z_at(offset), tensor)

    def remote(src, dst, send, recv, device):
        return pltpu.make_async_remote_copy(
            src_ref=src, dst_ref=dst, send_sem=send, recv_sem=recv, device_id=device, device_id_type=MESH
        )

    load_q = pltpu.make_async_copy(q_hbm, q_own, in_sem.at[0])
    load_order = pltpu.make_async_copy(order_hbm, order, in_sem.at[1])
    load_segment = pltpu.make_async_copy(segment_hbm, segment, in_sem.at[2])
    load_k = pltpu.make_async_copy(k_hbm, kbuf.at[at128(z)], in_sem.at[3])
    load_v = pltpu.make_async_copy(v_hbm, vbuf.at[at128(z)], in_sem.at[4])
    load_g = pltpu.make_async_copy(g_hbm, g_all.at[tensor], in_sem.at[5])
    load_w = pltpu.make_async_copy(w_hbm, w, in_sem.at[6])

    barrier = pltpu.get_barrier_semaphore()
    peers = [z_peer(d) for d in (1, -1, 2, -2, 3, -3)] + x_peer[1:] + y_peer[1:] + [partner]
    for peer in peers:
        pl.semaphore_signal(barrier, inc=1, device_id=peer, device_id_type=MESH)
    for load in (load_q, load_order, load_segment, load_k, load_v, load_g, load_w):
        load.start()

    pl.semaphore_wait(barrier, len(peers))

    def kv_copy(stream, sign, far):
        near = PARENT[far]
        src, buf = ((k_hbm, kbuf), (v_hbm, vbuf))[stream]
        slot = buf.at[at128(z_at(-sign * near))]
        at = sign * far + 8
        return remote(src if near == 0 else slot, slot, kv_s.at[stream, at], kv_r.at[stream, at], z_peer(sign * (far - near)))

    def kv_start(stream, *fars):
        for far in fars:
            for sign in SIGNS[far == 8, stream]:
                kv_copy(stream, sign, far).start()

    def kv_wait(stream, *fars):
        for far in fars:
            for sign in SIGNS[far == 8, stream]:
                kv_copy(stream, sign, far).wait_recv()

    def kv_relay(stream, far, *kids):
        for sign in (1, -1):
            kv_copy(stream, sign, far).wait_recv()
            for kid in kids:
                if sign in SIGNS[kid == 8, stream]:
                    kv_copy(stream, sign, kid).start()

    def q_copy(d):
        slot = q_t.at[:, at256(x)]
        return remote(slot, slot, q_s.at[d], q_r.at[d], x_peer[d])

    def do_copy(d):
        slot = do_t.at[:, at256(x)]
        return remote(slot, slot, do_s.at[d], do_r.at[d], x_peer[d])

    def gy_copy(d):
        return remote(g_hbm, g_all.at[tensor], gy_s.at[d], gy_r.at[d], y_peer[d])

    def gc_copy(d):
        at = y_at[d] * 2 + core
        return remote(g_hbm if d == 0 else g_all.at[at], g_all.at[at], gc_s.at[d], gc_r.at[d], partner)

    kv_start(0, 3)
    for d in range(1, ny):
        gy_copy(d).start()
    gc_copy(0).start()
    load_q.wait()
    for h in range(HEADS):
        q_t[:, at128(x * HEADS + h)] = q_own[:, h * HD : (h + 1) * HD].T
    for d in range(1, nx):
        q_copy(d).start()
    kv_start(0, 1)
    kv_start(1, 3, 1)

    load_order.wait()
    load_segment.wait()
    starts = [
        jnp.sum(jnp.where(segment[...] < d, 1, 0), axis=(0, 1), keepdims=True) for d in range(1, docs)
    ]
    for xp in range(nx):
        own = order[pl.ds(xp * nz + z, 1), :]
        first = jnp.zeros_like(own)
        for start in starts:
            first = jnp.maximum(first, jnp.where(start <= own, start, 0))
        pos_row[xp : xp + 1, :] = own
        pos_row[nx + xp : nx + xp + 1, :] = first

    @pl.loop(0, nz)
    def _(b):
        row = order[pl.ds(x * nz + b, 1), :]
        pos_key[at128(b), :] = jnp.broadcast_to(row, (ROWS, 128)).T

    top[...] = jnp.full_like(top, NEG)

    def stacked(ref, blocks):
        return jnp.concatenate([ref[at128(b), :] for b in blocks], axis=0)

    def score_blocks(*blocks):
        raw = mm(stacked(kbuf, blocks), q_t[...], NN)
        for i, b in enumerate(blocks):
            key = pos_key[at128(b), :]
            for xp in range(nx):
                mask = (key >= pos_row[nx + xp : nx + xp + 1, :]) & (key <= pos_row[xp : xp + 1, :])
                for h in range(HEADS):
                    lanes = slice((xp * HEADS + h) * 128, (xp * HEADS + h + 1) * 128)
                    part = jnp.where(mask, raw[i * ROWS : (i + 1) * ROWS, lanes], NEG)
                    scores[at128(b), lanes] = part
                    top[:, lanes] = jnp.maximum(top[:, lanes], jnp.max(part.reshape(ROWS // 8, 8, 128), axis=0))

    def sides(far):
        return z_at(-far), z_at(far)

    def score_far(*fars, wait=True):
        for far in fars:
            if wait:
                kv_wait(0, far)
            score_blocks(*sides(far))

    def cotangent_relay():
        for d in range(1, ny):
            gy_copy(d).wait_recv()
        for d in range(1, ny):
            gc_copy(d).start()

    def cotangent():
        load_w.wait()
        load_g.wait()
        for d in range(ny):
            gc_copy(d).wait_recv()
        acc = jnp.zeros((HEADS * HD, ROWS), F32)
        for t in range(2 * ny):
            acc = acc + mm(w[:, t * features : (t + 1) * features], g_all[t], NT)
        for h in range(HEADS):
            do_t[:, at128(x * HEADS + h)] = acc[h * HD : (h + 1) * HD, :].astype(BF)
        for d in range(1, nx):
            do_copy(d).start()

    kv_relay(0, 3, 6, 2, 4)
    load_k.wait()
    for d in range(1, nx):
        q_copy(d).wait_recv()
    kv_relay(1, 3, 6, 2, 4)
    score_blocks(z)
    score_far(3, wait=False)
    score_far(1)
    cotangent_relay()
    kv_relay(0, 6, 5, 7, 8)
    score_far(6, wait=False)
    score_far(2)
    kv_relay(1, 6, 5, 7, 8)
    cotangent()
    score_far(4, 5, 7)
    kv_wait(0, 8)
    score_blocks(z_at(-8))

    peak = jnp.max(top[...], axis=0, keepdims=True)
    total[...] = jnp.zeros_like(total)

    @pl.loop(0, nz)
    def _(i):
        p = jnp.exp2((scores[at128(i), :] - peak) * exponent)
        probs[at128(i), :] = p.astype(BF)
        total[...] += jnp.sum(p.reshape(16, 8, width), axis=0)

    sums = jnp.sum(total[...], axis=0, keepdims=True)
    for s in range(slots):
        lanes = slice(s * 128, (s + 1) * 128)
        stats[x, 0, s : s + 1, :] = peak[:, lanes]
        stats[x, 1, s : s + 1, :] = sums[:, lanes]

    def st_copy(d):
        return remote(stats.at[x], stats.at[x], st_s.at[d], st_r.at[d], x_peer[d])

    def in_copy(d):
        return remote(inners.at[x], inners.at[x], in_s.at[d], in_r.at[d], x_peer[d])

    def o_copy(d):
        return remote(o_send.at[:, at256(x_at[d])], o_recv.at[d], o_s.at[d], o_r.at[d], x_peer[d])

    for d in range(1, nx):
        st_copy(d).start()
    load_v.wait()
    kv_wait(1, 1, 2, 4, 5, 7, 8)
    o_t[...] = jnp.zeros_like(o_t)
    chunk = min(512, keys)

    @pl.loop(0, keys // chunk)
    def _(i):
        at = pl.ds(pl.multiple_of(i * chunk, chunk), chunk)
        o_t[...] += mm(vbuf[at, :], probs[at, :], TN)

    for d in range(1, nx):
        do_copy(d).wait_recv()
    inner = jnp.sum(o_t[...] * do_t[...].astype(F32), axis=0, keepdims=True)
    for s in range(slots):
        inners[x, s : s + 1, :] = inner[:, s * 128 : (s + 1) * 128]
    for d in range(1, nx):
        in_copy(d).start()
    o_send[...] = o_t[...].astype(BF)
    for d in range(1, nx):
        o_copy(d).start()
    for d in range(1, nx):
        st_copy(d).wait_recv()

    peak_all = functools.reduce(jnp.maximum, [stats[i, 0] for i in range(nx)])
    weight = [jnp.exp2((stats[i, 0] - peak_all) * exponent) for i in range(nx)]
    inverse = 1.0 / functools.reduce(jnp.add, [weight[i] * stats[i, 1] for i in range(nx)])
    for i in range(nx):
        factor[i] = weight[i] * inverse
    mine = factor[x]
    for s in range(slots):
        lanes = slice(s * 128, (s + 1) * 128)
        f = mine[s : s + 1, :]
        fdo_t[:, lanes] = (do_t[:, lanes].astype(F32) * f).astype(BF)
        fq_t[:, lanes] = (q_t[:, lanes].astype(F32) * (f * scale)).astype(BF)

    def rs_copy(stream, sign, far):
        at = sign * far + 8
        return remote(
            rs_send.at[stream, at], rs_recv.at[stream, at], rs_s.at[stream, at], rs_r.at[stream, at],
            z_peer(sign * (UP[stream][far] - far)),
        )

    def rs_out(stream, sign, far, *kids):
        acc = (dk_part, dv_part)[stream][z_at(-sign * far)]
        for kid in kids:
            rs_copy(stream, sign, kid).wait_recv()
            acc = acc + rs_recv[stream, sign * kid + 8].astype(F32)
        rs_send[stream, sign * far + 8] = acc.astype(BF)
        rs_copy(stream, sign, far).start()

    def rs_hubs(stream, far):
        for sign in (1, -1):
            kids = [kid for kid in UP[stream] if UP[stream][kid] == far]
            rs_out(stream, sign, far, *[kid for kid in kids if sign in SIGNS[kid == 8, stream]])

    def dv_blocks(*blocks):
        part = mm(stacked(probs, blocks), fdo_t[...], NT)
        for i, b in enumerate(blocks):
            dv_part[b] = part[i * ROWS : (i + 1) * ROWS, :]

    def ds_blocks(*blocks):
        dp = mm(stacked(vbuf, blocks), do_t[...], NN)
        for i, b in enumerate(blocks):
            for s in range(slots):
                lanes = slice(s * 128, (s + 1) * 128)
                p = probs[at128(b), lanes].astype(F32)
                diff = dp[i * ROWS : (i + 1) * ROWS, lanes] - delta[s : s + 1, :]
                dscores[at128(b), lanes] = (p * diff).astype(BF)
        ds = stacked(dscores, blocks)
        part = mm(ds, fq_t[...], NT)
        for i, b in enumerate(blocks):
            dk_part[b] = part[i * ROWS : (i + 1) * ROWS, :]
        dq_t[...] += mm(stacked(kbuf, blocks), ds, TN)

    def grad_far(stream, *fars):
        for far in fars:
            (ds_blocks, dv_blocks)[stream](*sides(far))
            if far in LEAVES:
                for sign in (1, -1):
                    rs_out(stream, sign, far)

    def grad_antipode(stream):
        (ds_blocks, dv_blocks)[stream](z_at(-8))
        rs_out(stream, SIGNS[True, stream][0], 8)

    grad_far(1, 5, 7)
    grad_antipode(1)
    grad_far(1, 2, 4, 1, 6, 3)
    dv_blocks(z)
    dq_t[...] = jnp.zeros_like(dq_t)
    for d in range(1, nx):
        in_copy(d).wait_recv()
    delta[...] = functools.reduce(jnp.add, [factor[i] * inners[i] for i in range(nx)])

    def dq_copy(d):
        return remote(dq_send.at[:, at256(x_at[d])], dq_recv.at[d], dq_s.at[d], dq_r.at[d], x_peer[d])

    def pc_copy():
        return remote(part_send, part_recv, pc_s.at[0], pc_r.at[0], partner)

    def py_copy(d):
        return remote(y_send.at[y_at[d]], y_recv.at[d], py_s.at[d], py_r.at[d], y_peer[d])

    def project():
        for d in range(1, nx):
            o_copy(d).wait_recv()
        attended = []
        for h in range(HEADS):
            acc = o_send[:, at128(x * HEADS + h)].astype(F32) * factor[x, pl.ds(x * HEADS + h, 1), :]
            for d in range(1, nx):
                source = lax.rem(x - d + nx, nx)
                acc = acc + (
                    o_recv[d, :, h * 128 : (h + 1) * 128].astype(F32) * factor[source, pl.ds(x * HEADS + h, 1), :]
                )
            attended.append(acc.astype(BF))
        attended = jnp.concatenate(attended, axis=0)

        @pl.loop(0, ny)
        def _(yp):
            for c in range(2):
                at = pl.ds(pl.multiple_of((yp * 2 + c) * features, features), features)
                part = mm(attended, w[:, at], TN)

                @pl.when(core == c)
                def _():
                    part_own[yp] = part

                @pl.when(core != c)
                def _():
                    part_send[yp] = part.astype(BF)

        pc_copy().start()

    def spread():
        pc_copy().wait_recv()

        @pl.loop(0, ny)
        def _(yp):
            part = part_own[yp] + part_recv[yp].astype(F32)
            part_own[yp] = part
            y_send[yp] = part.astype(BF)

        for d in range(1, ny):
            py_copy(d).start()

    def send_dq():
        for s in range(slots):
            lanes = slice(s * 128, (s + 1) * 128)
            dq_t[:, lanes] = dq_t[:, lanes] * (factor[x, s : s + 1, :] * scale)
        dq_send[...] = dq_t[...].astype(BF)
        for d in range(1, nx):
            dq_copy(d).start()

    grad_far(0, 5, 7)
    grad_antipode(0)
    rs_hubs(1, 6)
    grad_far(0, 2, 4)
    project()
    grad_far(0, 6)
    rs_hubs(0, 6)
    grad_far(0, 3, 1)
    ds_blocks(z)
    send_dq()
    spread()
    rs_hubs(1, 3)
    rs_hubs(0, 3)

    def owned(part, stream):
        acc = part[z]
        for far in [far for far in UP[stream] if UP[stream][far] == 0]:
            for sign in (1, -1):
                rs_copy(stream, sign, far).wait_recv()
                acc = acc + rs_recv[stream, sign * far + 8].astype(F32)
        return acc.astype(BF)

    dv_v[...] = owned(dv_part, 1)
    for d in range(1, nx):
        dq_copy(d).wait_recv()
    for h in range(HEADS):
        acc = dq_t[:, at128(x * HEADS + h)]
        for d in range(1, nx):
            acc = acc + dq_recv[d, :, h * 128 : (h + 1) * 128].astype(F32)
        dq_v[:, h * 128 : (h + 1) * 128] = acc.T.astype(BF)
    for d in range(1, ny):
        py_copy(d).wait_recv()
    out = part_own[y]
    for d in range(1, ny):
        out = out + y_recv[d].astype(F32)
    out_v[...] = out.astype(BF)
    dk_v[...] = owned(dk_part, 0)

    for stream in range(2):
        for far in PARENT:
            for sign in SIGNS[far == 8, stream]:
                kv_copy(stream, sign, far).wait_send()
                rs_copy(stream, sign, far).wait_send()
    for d in range(1, nx):
        for copy in (q_copy, do_copy, st_copy, in_copy, o_copy, dq_copy):
            copy(d).wait_send()
    for d in range(1, ny):
        gy_copy(d).wait_send()
        py_copy(d).wait_send()
    for d in range(ny):
        gc_copy(d).wait_send()
    pc_copy().wait_send()


def per_device(nx, nz, ny, docs, query, key_proj, value, out_weight, grad_out, order, segment):
    features = grad_out.shape[1]
    keys, width, slots = nz * ROWS, nx * HEADS * 128, nx * HEADS
    tokens = order.shape[0]
    order = order.reshape(tokens // 128, 128)
    segment = segment.reshape(tokens // 128, 128)

    def vm(*shape, dtype=BF):
        return pltpu.VMEM(shape, dtype)

    def sem(*shape):
        return pltpu.SemaphoreType.DMA(shape)

    scratch = [
        vm(ROWS, HEADS * HD), vm(HEADS * HD, out_weight.shape[1]),
        vm(tokens // 128, 128, dtype=jnp.int32), vm(tokens // 128, 128, dtype=jnp.int32),
        vm(keys, HD), vm(keys, HD), vm(HD, width), vm(HD, width), vm(2 * ny, ROWS, features),
        vm(2 * nx, 128, dtype=jnp.int32), vm(keys, 128, dtype=jnp.int32),
        vm(keys, width, dtype=F32), vm(keys, width), vm(keys, width),
        vm(8, width, dtype=F32), vm(8, width, dtype=F32), vm(HD, width, dtype=F32), vm(HD, width, dtype=F32),
        vm(nx, 2, slots, 128, dtype=F32), vm(nx, slots, 128, dtype=F32), vm(HD, width), vm(nx, HD, 256),
        vm(nx, slots, 128, dtype=F32), vm(slots, 128, dtype=F32), vm(HD, width), vm(HD, width),
        vm(nz, ROWS, HD, dtype=F32), vm(nz, ROWS, HD, dtype=F32),
        vm(2, 17, ROWS, HD), vm(2, 17, ROWS, HD), vm(HD, width), vm(nx, HD, 256),
        vm(ny, ROWS, features, dtype=F32), vm(ny, ROWS, features), vm(ny, ROWS, features),
        vm(ny, ROWS, features), vm(ny, ROWS, features),
        sem(7), sem(2, 17), sem(2, 17),
    ] + [sem(nx)] * 12 + [sem(ny)] * 4 + [sem(1)] * 2 + [sem(ny)] * 2 + [sem(2, 17)] * 2
    args = (query, key_proj, value, out_weight, grad_out, order, segment)
    flops = 2 * width * keys * HD * 6 + 4 * ROWS * HEADS * HD * out_weight.shape[1]
    return pl.pallas_call(
        functools.partial(kernel, nx, nz, ny, docs),
        out_shape=[
            pltpu.VMEM((ROWS, features), BF),
            pltpu.VMEM((ROWS, HEADS * HD), BF),
            pltpu.VMEM((ROWS, HD), BF),
            pltpu.VMEM((ROWS, HD), BF),
        ],
        in_specs=[pl.BlockSpec(memory_space=pltpu.HBM)] * 7,
        out_specs=[pl.BlockSpec(memory_space=pltpu.VMEM)] * 4,
        scratch_shapes=scratch,
        compiler_params=pltpu.CompilerParams(
            collective_id=0, has_side_effects=True, vmem_limit_bytes=56 * 1024 * 1024
        ),
        cost_estimate=pl.CostEstimate(flops=flops, bytes_accessed=4 << 20, transcendentals=keys * width),
    )(*[pltpu.with_memory_space_constraint(a, pltpu.HBM) for a in args])


def solution(mesh):
    nx, nz = FACTORS[mesh.shape["context"]]
    ny = mesh.shape["tensor"] // 2
    return jax.shard_map(
        functools.partial(per_device, nx, nz, ny, 8),
        mesh=mesh,
        in_specs=(
            P("context", "tensor"),
            P("context", "tensor"),
            P("context", "tensor"),
            P("tensor", None),
            P("context", "tensor"),
            P(),
            P(),
        ),
        out_specs=(P("context", "tensor"),) * 4,
        check_vma=False,
    )
```

```python
import functools
import math

import jax
import jax.numpy as jnp
from jax import lax
from jax.experimental import pallas as pl
from jax.experimental.pallas import tpu as pltpu
from jax.sharding import PartitionSpec as P

MESH = pl.DeviceIdType.MESH
NEG = -1e30
HD = 128
ROWS = 128
HEADS = 2
BF = jnp.bfloat16
F32 = jnp.float32
FACTORS = {64: (4, 16)}
PARENT = {3: 0, 1: 0, 6: 3, 2: 3, 4: 3, 5: 6, 7: 6, 8: 6}
UP = (PARENT, PARENT)
LEAVES = (1, 2, 4, 5, 7, 8)
SIGNS = {(False, 0): (1, -1), (False, 1): (1, -1), (True, 0): (1,), (True, 1): (-1,)}

NN = (((1,), (0,)), ((), ()))
NT = (((1,), (1,)), ((), ()))
TN = (((0,), (0,)), ((), ()))


def mm(a, b, dims):
    return lax.dot_general(a, b, dims, preferred_element_type=F32)


def at128(index):
    return pl.ds(pl.multiple_of(index * 128, 128), 128)


def at256(index):
    return pl.ds(pl.multiple_of(index * 256, 256), 256)


def kernel(
    nx, nz, ny, docs,
    q_hbm, k_hbm, v_hbm, w_hbm, g_hbm, order_hbm, segment_hbm,
    out_v, dq_v, dk_v, dv_v,
    q_own, w, order, segment, kbuf, vbuf, q_t, do_t, g_all,
    pos_row, pos_key, scores, probs, dscores, top, total, o_t, dq_t,
    stats, inners, o_send, o_recv, factor, delta, fdo_t, fq_t,
    dk_part, dv_part, rs_send, rs_recv, dq_send, dq_recv,
    part_own, part_send, part_recv, y_send, y_recv,
    in_sem, kv_s, kv_r, q_s, q_r, do_s, do_r, st_s, st_r, in_s, in_r, o_s, o_r, dq_s, dq_r,
    gy_s, gy_r, gc_s, gc_r, pc_s, pc_r, py_s, py_r, rs_s, rs_r,
):
    context, tensor = lax.axis_index("context"), lax.axis_index("tensor")
    x, z = context // nz, lax.rem(context, nz)
    y, core = tensor // 2, lax.rem(tensor, 2)
    exponent = math.log2(math.e) / math.sqrt(HD)
    scale = 1.0 / math.sqrt(HD)
    slots = nx * HEADS
    width = slots * 128
    keys = nz * ROWS
    features = g_hbm.shape[1]
    x_at = [lax.rem(x + d, nx) for d in range(nx)]
    x_peer = [(x_at[d] * nz + z, tensor) for d in range(nx)]
    y_at = [lax.rem(y + d, ny) for d in range(ny)]
    y_peer = [(context, y_at[d] * 2 + core) for d in range(ny)]
    partner = (context, y * 2 + 1 - core)

    def z_at(offset):
        return lax.rem(z + offset + 2 * nz, nz)

    def z_peer(offset):
        return (x * nz + z_at(offset), tensor)

    def remote(src, dst, send, recv, device):
        return pltpu.make_async_remote_copy(
            src_ref=src, dst_ref=dst, send_sem=send, recv_sem=recv, device_id=device, device_id_type=MESH
        )

    load_q = pltpu.make_async_copy(q_hbm, q_own, in_sem.at[0])
    load_order = pltpu.make_async_copy(order_hbm, order, in_sem.at[1])
    load_segment = pltpu.make_async_copy(segment_hbm, segment, in_sem.at[2])
    load_k = pltpu.make_async_copy(k_hbm, kbuf.at[at128(z)], in_sem.at[3])
    load_v = pltpu.make_async_copy(v_hbm, vbuf.at[at128(z)], in_sem.at[4])
    load_g = pltpu.make_async_copy(g_hbm, g_all.at[tensor], in_sem.at[5])
    load_w = pltpu.make_async_copy(w_hbm, w, in_sem.at[6])

    barrier = pltpu.get_barrier_semaphore()
    peers = [z_peer(d) for d in (1, -1, 2, -2, 3, -3)] + x_peer[1:] + y_peer[1:] + [partner]
    for peer in peers:
        pl.semaphore_signal(barrier, inc=1, device_id=peer, device_id_type=MESH)
    for load in (load_q, load_order, load_segment, load_k, load_v, load_g, load_w):
        load.start()

    pl.semaphore_wait(barrier, len(peers))

    def kv_copy(stream, sign, far):
        near = PARENT[far]
        src, buf = ((k_hbm, kbuf), (v_hbm, vbuf))[stream]
        slot = buf.at[at128(z_at(-sign * near))]
        at = sign * far + 8
        return remote(src if near == 0 else slot, slot, kv_s.at[stream, at], kv_r.at[stream, at], z_peer(sign * (far - near)))

    def kv_start(stream, *fars):
        for far in fars:
            for sign in SIGNS[far == 8, stream]:
                kv_copy(stream, sign, far).start()

    def kv_wait(stream, *fars):
        for far in fars:
            for sign in SIGNS[far == 8, stream]:
                kv_copy(stream, sign, far).wait_recv()

    def kv_relay(stream, far, *kids):
        for sign in (1, -1):
            kv_copy(stream, sign, far).wait_recv()
            for kid in kids:
                if sign in SIGNS[kid == 8, stream]:
                    kv_copy(stream, sign, kid).start()

    def q_copy(d):
        slot = q_t.at[:, at256(x)]
        return remote(slot, slot, q_s.at[d], q_r.at[d], x_peer[d])

    def do_copy(d):
        slot = do_t.at[:, at256(x)]
        return remote(slot, slot, do_s.at[d], do_r.at[d], x_peer[d])

    def gy_copy(d):
        return remote(g_hbm, g_all.at[tensor], gy_s.at[d], gy_r.at[d], y_peer[d])

    def gc_copy(d):
        at = y_at[d] * 2 + core
        return remote(g_hbm if d == 0 else g_all.at[at], g_all.at[at], gc_s.at[d], gc_r.at[d], partner)

    kv_start(0, 3)
    for d in range(1, ny):
        gy_copy(d).start()
    gc_copy(0).start()
    load_q.wait()
    for h in range(HEADS):
        q_t[:, at128(x * HEADS + h)] = q_own[:, h * HD : (h + 1) * HD].T
    for d in range(1, nx):
        q_copy(d).start()
    kv_start(1, 3)

    load_order.wait()
    load_segment.wait()
    starts = [
        jnp.sum(jnp.where(segment[...] < d, 1, 0), axis=(0, 1), keepdims=True) for d in range(1, docs)
    ]
    for xp in range(nx):
        own = order[pl.ds(xp * nz + z, 1), :]
        first = jnp.zeros_like(own)
        for start in starts:
            first = jnp.maximum(first, jnp.where(start <= own, start, 0))
        pos_row[xp : xp + 1, :] = own
        pos_row[nx + xp : nx + xp + 1, :] = first

    @pl.loop(0, nz)
    def _(b):
        row = order[pl.ds(x * nz + b, 1), :]
        pos_key[at128(b), :] = jnp.broadcast_to(row, (ROWS, 128)).T

    top[...] = jnp.full_like(top, NEG)

    def stacked(ref, blocks):
        return jnp.concatenate([ref[at128(b), :] for b in blocks], axis=0)

    def score_blocks(*blocks):
        raw = mm(stacked(kbuf, blocks), q_t[...], NN)
        for i, b in enumerate(blocks):
            key = pos_key[at128(b), :]
            for xp in range(nx):
                mask = (key >= pos_row[nx + xp : nx + xp + 1, :]) & (key <= pos_row[xp : xp + 1, :])
                for h in range(HEADS):
                    lanes = slice((xp * HEADS + h) * 128, (xp * HEADS + h + 1) * 128)
                    part = jnp.where(mask, raw[i * ROWS : (i + 1) * ROWS, lanes], NEG)
                    scores[at128(b), lanes] = part
                    top[:, lanes] = jnp.maximum(top[:, lanes], jnp.max(part.reshape(ROWS // 8, 8, 128), axis=0))

    def sides(far):
        return z_at(-far), z_at(far)

    def score_far(*fars, wait=True):
        for far in fars:
            if wait:
                kv_wait(0, far)
            score_blocks(*sides(far))

    def cotangent_relay():
        for d in range(1, ny):
            gy_copy(d).wait_recv()
        for d in range(1, ny):
            gc_copy(d).start()

    def cotangent():
        load_w.wait()
        load_g.wait()
        for d in range(ny):
            gc_copy(d).wait_recv()
        acc = jnp.zeros((HEADS * HD, ROWS), F32)
        for t in range(2 * ny):
            acc = acc + mm(w[:, t * features : (t + 1) * features], g_all[t], NT)
        for h in range(HEADS):
            do_t[:, at128(x * HEADS + h)] = acc[h * HD : (h + 1) * HD, :].astype(BF)
        for d in range(1, nx):
            do_copy(d).start()

    kv_relay(0, 3, 6, 2, 4)
    load_k.wait()
    for d in range(1, nx):
        q_copy(d).wait_recv()
    kv_relay(1, 3, 6, 2, 4)
    kv_start(0, 1)
    kv_start(1, 1)
    score_blocks(z)
    score_far(3, wait=False)
    cotangent_relay()
    kv_relay(0, 6, 5, 7, 8)
    score_far(6, wait=False)
    score_far(2)
    kv_relay(1, 6, 5, 7, 8)
    score_far(1)
    cotangent()
    score_far(4, 5, 7)
    kv_wait(0, 8)
    score_blocks(z_at(-8))

    peak = jnp.max(top[...], axis=0, keepdims=True)
    total[...] = jnp.zeros_like(total)

    @pl.loop(0, nz)
    def _(i):
        p = jnp.exp2((scores[at128(i), :] - peak) * exponent)
        probs[at128(i), :] = p.astype(BF)
        total[...] += jnp.sum(p.reshape(16, 8, width), axis=0)

    sums = jnp.sum(total[...], axis=0, keepdims=True)
    for s in range(slots):
        lanes = slice(s * 128, (s + 1) * 128)
        stats[x, 0, s : s + 1, :] = peak[:, lanes]
        stats[x, 1, s : s + 1, :] = sums[:, lanes]

    def st_copy(d):
        return remote(stats.at[x], stats.at[x], st_s.at[d], st_r.at[d], x_peer[d])

    def in_copy(d):
        return remote(inners.at[x], inners.at[x], in_s.at[d], in_r.at[d], x_peer[d])

    def o_copy(d):
        return remote(o_send.at[:, at256(x_at[d])], o_recv.at[d], o_s.at[d], o_r.at[d], x_peer[d])

    for d in range(1, nx):
        st_copy(d).start()
    load_v.wait()
    kv_wait(1, 1, 2, 4, 5, 7, 8)
    o_t[...] = jnp.zeros_like(o_t)
    chunk = min(512, keys)

    @pl.loop(0, keys // chunk)
    def _(i):
        at = pl.ds(pl.multiple_of(i * chunk, chunk), chunk)
        o_t[...] += mm(vbuf[at, :], probs[at, :], TN)

    for d in range(1, nx):
        do_copy(d).wait_recv()
    inner = jnp.sum(o_t[...] * do_t[...].astype(F32), axis=0, keepdims=True)
    for s in range(slots):
        inners[x, s : s + 1, :] = inner[:, s * 128 : (s + 1) * 128]
    for d in range(1, nx):
        in_copy(d).start()
    o_send[...] = o_t[...].astype(BF)
    for d in range(1, nx):
        o_copy(d).start()
    for d in range(1, nx):
        st_copy(d).wait_recv()

    peak_all = functools.reduce(jnp.maximum, [stats[i, 0] for i in range(nx)])
    weight = [jnp.exp2((stats[i, 0] - peak_all) * exponent) for i in range(nx)]
    inverse = 1.0 / functools.reduce(jnp.add, [weight[i] * stats[i, 1] for i in range(nx)])
    for i in range(nx):
        factor[i] = weight[i] * inverse
    mine = factor[x]
    for s in range(slots):
        lanes = slice(s * 128, (s + 1) * 128)
        f = mine[s : s + 1, :]
        fdo_t[:, lanes] = (do_t[:, lanes].astype(F32) * f).astype(BF)
        fq_t[:, lanes] = (q_t[:, lanes].astype(F32) * (f * scale)).astype(BF)

    def rs_copy(stream, sign, far):
        at = sign * far + 8
        return remote(
            rs_send.at[stream, at], rs_recv.at[stream, at], rs_s.at[stream, at], rs_r.at[stream, at],
            z_peer(sign * (UP[stream][far] - far)),
        )

    def rs_out(stream, sign, far, *kids):
        acc = (dk_part, dv_part)[stream][z_at(-sign * far)]
        for kid in kids:
            rs_copy(stream, sign, kid).wait_recv()
            acc = acc + rs_recv[stream, sign * kid + 8].astype(F32)
        rs_send[stream, sign * far + 8] = acc.astype(BF)
        rs_copy(stream, sign, far).start()

    def rs_hubs(stream, far):
        for sign in (1, -1):
            kids = [kid for kid in UP[stream] if UP[stream][kid] == far]
            rs_out(stream, sign, far, *[kid for kid in kids if sign in SIGNS[kid == 8, stream]])

    def dv_blocks(*blocks):
        part = mm(stacked(probs, blocks), fdo_t[...], NT)
        for i, b in enumerate(blocks):
            dv_part[b] = part[i * ROWS : (i + 1) * ROWS, :]

    def ds_blocks(*blocks):
        dp = mm(stacked(vbuf, blocks), do_t[...], NN)
        for i, b in enumerate(blocks):
            for s in range(slots):
                lanes = slice(s * 128, (s + 1) * 128)
                p = probs[at128(b), lanes].astype(F32)
                diff = dp[i * ROWS : (i + 1) * ROWS, lanes] - delta[s : s + 1, :]
                dscores[at128(b), lanes] = (p * diff).astype(BF)
        ds = stacked(dscores, blocks)
        part = mm(ds, fq_t[...], NT)
        for i, b in enumerate(blocks):
            dk_part[b] = part[i * ROWS : (i + 1) * ROWS, :]
        dq_t[...] += mm(stacked(kbuf, blocks), ds, TN)

    def grad_far(stream, *fars):
        for far in fars:
            (ds_blocks, dv_blocks)[stream](*sides(far))
            if far in LEAVES:
                for sign in (1, -1):
                    rs_out(stream, sign, far)

    def grad_antipode(stream):
        (ds_blocks, dv_blocks)[stream](z_at(-8))
        rs_out(stream, SIGNS[True, stream][0], 8)

    grad_far(1, 5, 7)
    grad_antipode(1)
    dq_t[...] = jnp.zeros_like(dq_t)
    for d in range(1, nx):
        in_copy(d).wait_recv()
    delta[...] = functools.reduce(jnp.add, [factor[i] * inners[i] for i in range(nx)])

    def dq_copy(d):
        return remote(dq_send.at[:, at256(x_at[d])], dq_recv.at[d], dq_s.at[d], dq_r.at[d], x_peer[d])

    far_first = sorted(range(1, ny), key=lambda d: -min(d, ny - d)) + [0]

    def pc_copy(d):
        return remote(part_send.at[d], part_recv.at[d], pc_s.at[d], pc_r.at[d], partner)

    def py_copy(d):
        return remote(y_send.at[d], y_recv.at[d], py_s.at[d], py_r.at[d], y_peer[d])

    def project():
        for d in range(1, nx):
            o_copy(d).wait_recv()
        attended = []
        for h in range(HEADS):
            acc = o_send[:, at128(x * HEADS + h)].astype(F32) * factor[x, pl.ds(x * HEADS + h, 1), :]
            for d in range(1, nx):
                source = lax.rem(x - d + nx, nx)
                acc = acc + (
                    o_recv[d, :, h * 128 : (h + 1) * 128].astype(F32) * factor[source, pl.ds(x * HEADS + h, 1), :]
                )
            attended.append(acc.astype(BF))
        attended = jnp.concatenate(attended, axis=0)

        for d in far_first:
            other = pl.ds(pl.multiple_of((y_at[d] * 2 + 1 - core) * features, features), features)
            part_send[d] = mm(attended, w[:, other], TN).astype(BF)
            pc_copy(d).start()
            own = pl.ds(pl.multiple_of((y_at[d] * 2 + core) * features, features), features)
            part_own[d] = mm(attended, w[:, own], TN)

    def spread():
        for d in far_first:
            pc_copy(d).wait_recv()
            part = part_own[d] + part_recv[d].astype(F32)
            if d == 0:
                part_own[d] = part
            else:
                y_send[d] = part.astype(BF)
                py_copy(d).start()

    def send_dq():
        for s in range(slots):
            lanes = slice(s * 128, (s + 1) * 128)
            dq_t[:, lanes] = dq_t[:, lanes] * (factor[x, s : s + 1, :] * scale)
        dq_send[...] = dq_t[...].astype(BF)
        for d in range(1, nx):
            dq_copy(d).start()

    grad_far(0, 5, 7)
    grad_antipode(0)
    grad_far(1, 2, 4, 6)
    rs_hubs(1, 6)
    grad_far(0, 2, 4)
    project()
    grad_far(0, 6)
    rs_hubs(0, 6)
    grad_far(1, 1, 3)
    dv_blocks(z)
    grad_far(0, 1, 3)
    ds_blocks(z)
    send_dq()
    spread()
    rs_hubs(1, 3)
    rs_hubs(0, 3)

    def owned(part, stream):
        acc = part[z]
        for far in [far for far in UP[stream] if UP[stream][far] == 0]:
            for sign in (1, -1):
                rs_copy(stream, sign, far).wait_recv()
                acc = acc + rs_recv[stream, sign * far + 8].astype(F32)
        return acc.astype(BF)

    dv_v[...] = owned(dv_part, 1)
    for d in range(1, nx):
        dq_copy(d).wait_recv()
    for h in range(HEADS):
        acc = dq_t[:, at128(x * HEADS + h)]
        for d in range(1, nx):
            acc = acc + dq_recv[d, :, h * 128 : (h + 1) * 128].astype(F32)
        dq_v[:, h * 128 : (h + 1) * 128] = acc.T.astype(BF)
    for d in range(1, ny):
        py_copy(d).wait_recv()
    out = part_own[0]
    for d in range(1, ny):
        out = out + y_recv[d].astype(F32)
    out_v[...] = out.astype(BF)
    dk_v[...] = owned(dk_part, 0)

    for stream in range(2):
        for far in PARENT:
            for sign in SIGNS[far == 8, stream]:
                kv_copy(stream, sign, far).wait_send()
                rs_copy(stream, sign, far).wait_send()
    for d in range(1, nx):
        for copy in (q_copy, do_copy, st_copy, in_copy, o_copy, dq_copy):
            copy(d).wait_send()
    for d in range(1, ny):
        gy_copy(d).wait_send()
        py_copy(d).wait_send()
    for d in range(ny):
        gc_copy(d).wait_send()
        pc_copy(d).wait_send()


def per_device(nx, nz, ny, docs, query, key_proj, value, out_weight, grad_out, order, segment):
    features = grad_out.shape[1]
    keys, width, slots = nz * ROWS, nx * HEADS * 128, nx * HEADS
    tokens = order.shape[0]
    order = order.reshape(tokens // 128, 128)
    segment = segment.reshape(tokens // 128, 128)

    def vm(*shape, dtype=BF):
        return pltpu.VMEM(shape, dtype)

    def sem(*shape):
        return pltpu.SemaphoreType.DMA(shape)

    scratch = [
        vm(ROWS, HEADS * HD), vm(HEADS * HD, out_weight.shape[1]),
        vm(tokens // 128, 128, dtype=jnp.int32), vm(tokens // 128, 128, dtype=jnp.int32),
        vm(keys, HD), vm(keys, HD), vm(HD, width), vm(HD, width), vm(2 * ny, ROWS, features),
        vm(2 * nx, 128, dtype=jnp.int32), vm(keys, 128, dtype=jnp.int32),
        vm(keys, width, dtype=F32), vm(keys, width), vm(keys, width),
        vm(8, width, dtype=F32), vm(8, width, dtype=F32), vm(HD, width, dtype=F32), vm(HD, width, dtype=F32),
        vm(nx, 2, slots, 128, dtype=F32), vm(nx, slots, 128, dtype=F32), vm(HD, width), vm(nx, HD, 256),
        vm(nx, slots, 128, dtype=F32), vm(slots, 128, dtype=F32), vm(HD, width), vm(HD, width),
        vm(nz, ROWS, HD, dtype=F32), vm(nz, ROWS, HD, dtype=F32),
        vm(2, 17, ROWS, HD), vm(2, 17, ROWS, HD), vm(HD, width), vm(nx, HD, 256),
        vm(ny, ROWS, features, dtype=F32), vm(ny, ROWS, features), vm(ny, ROWS, features),
        vm(ny, ROWS, features), vm(ny, ROWS, features),
        sem(7), sem(2, 17), sem(2, 17),
    ] + [sem(nx)] * 12 + [sem(ny)] * 8 + [sem(2, 17)] * 2
    args = (query, key_proj, value, out_weight, grad_out, order, segment)
    flops = 2 * width * keys * HD * 6 + 4 * ROWS * HEADS * HD * out_weight.shape[1]
    return pl.pallas_call(
        functools.partial(kernel, nx, nz, ny, docs),
        out_shape=[
            pltpu.VMEM((ROWS, features), BF),
            pltpu.VMEM((ROWS, HEADS * HD), BF),
            pltpu.VMEM((ROWS, HD), BF),
            pltpu.VMEM((ROWS, HD), BF),
        ],
        in_specs=[pl.BlockSpec(memory_space=pltpu.HBM)] * 7,
        out_specs=[pl.BlockSpec(memory_space=pltpu.VMEM)] * 4,
        scratch_shapes=scratch,
        compiler_params=pltpu.CompilerParams(
            collective_id=0, has_side_effects=True, vmem_limit_bytes=56 * 1024 * 1024
        ),
        cost_estimate=pl.CostEstimate(flops=flops, bytes_accessed=4 << 20, transcendentals=keys * width),
    )(*[pltpu.with_memory_space_constraint(a, pltpu.HBM) for a in args])


def solution(mesh):
    nx, nz = FACTORS[mesh.shape["context"]]
    ny = mesh.shape["tensor"] // 2
    return jax.shard_map(
        functools.partial(per_device, nx, nz, ny, 8),
        mesh=mesh,
        in_specs=(
            P("context", "tensor"),
            P("context", "tensor"),
            P("context", "tensor"),
            P("tensor", None),
            P("context", "tensor"),
            P(),
            P(),
        ),
        out_specs=(P("context", "tensor"),) * 4,
        check_vma=False,
    )
```
